512 devices in a mesh: seq: 64 (over x, y, core), mp: 8 (over z).
Axes of the slice: x: 4, y: 8, z: 8, core: 2. Of those that a mesh axis runs over, the one named last changes fastest.
Arguments:
- token_ids: int32 [96, 2], replicated, may hold values from 0 to 25599
- prompt_lengths: int32 [6], replicated, may hold values from 1024 to 8192, as said below
- tail_lengths: int32 [96], replicated, may hold values from 32 to 256, as said below
- prompt_of: int32 [96], replicated, may hold values from 0 to 5, as said below
- page_table: int32 [96, 2], replicated, may hold values from 0 to 191, as said below
- prompt_keys: bfloat16 [49152, 6144], P('seq', 'mp'), may hold values from -240 to 240
- prompt_values: bfloat16 [49152, 6144], P('seq', 'mp'), may hold values from -12 to 12
- tail_keys: bfloat16 [24576, 6144], P('seq', 'mp'), may hold values from -240 to 240
- tail_values: bfloat16 [24576, 6144], P('seq', 'mp'), may hold values from -12 to 12
- norm_gain: bfloat16 [2, 7168], P(None, 'seq'), may hold values from 0.5 to 1.5
- norm_bias: bfloat16 [2, 7168], P(None, 'seq'), may hold values from -2 to 2
- qkv_weight: bfloat16 [7168, 3, 6144], P('seq', None, 'mp'), may hold values from -0.0625 to 0.0625
- qkv_bias: bfloat16 [3, 6144], P(None, 'mp'), may hold values from -2 to 2
- out_weight: bfloat16 [6144, 7168], P('mp', 'seq'), may hold values from -0.078125 to 0.078125
- out_bias: bfloat16 [7168], P('seq'), may hold values from -0.796875 to 0.796875
- embedding: bfloat16 [25600, 7168], P('mp', 'seq'), may hold values from -0.3984375 to 0.3984375
- score_weight: bfloat16 [7168], P('seq'), may hold values from -0.0625 to 0.0625
Outputs:
- hidden_states: bfloat16 [192, 7168], P(None, 'seq')
- score_values: float32 [96], replicated
- hidden_norms: float32 [192], replicated
- top_logits: float32 [96], replicated
The draws below stay inside these ranges and needn't reach their ends.
Inputs may be any that keep to these rules, and one draw needn't show every extreme that they name: `prompt_lengths`: the longest prompt has exactly 8192 positions. `tail_lengths`: some continuation has exactly 256 tail tokens. `prompt_of`: each prompt is extended by 16 continuations or one more. `page_table`: all entries are distinct, so every pool page belongs to one continuation.
All inputs are finite; a program needn't handle non-finite values.
Results may differ from the reference program's by a relative error of at most 0.017.
The reference program's roundings to bfloat16 on the way (of `embedded`, `normed`, `qkv`, `weights`, `attended` and `final`) count: a program that leaves them out, or rounds other values in their place, can miss the bound.
Values may be sent and summed in bfloat16 or wider, within the bound.
A program may use at most 128 MiB of HBM per device.

```python
import math
import jax
import jax.numpy as jnp
import numpy as np
from jax import lax

D = 7168
HD = 128
HEADS = 48
VOCAB = 25600
NPROMPT = 6
PAGE = 128
CACHE = 49152
PMOST = 8192
POOL = 192
CONT = 96
ROWS = 192
TAIL_MAX = 256
TAIL_MIN = 32


def spiky_keys(key, count):
    first = jax.random.fold_in(key, 0)
    return jnp.clip(jax.random.normal(first, (count, HEADS * HD), jnp.float32) * 1.5, -9.0, 9.0)


def draw_prompt_keys(key, part):
    return spiky_keys(jax.random.fold_in(key, 11), CACHE).astype(jnp.bfloat16)


def draw_tail_keys(key, part):
    return spiky_keys(jax.random.fold_in(key, 13), POOL * PAGE).astype(jnp.bfloat16)


def draw_prompt_lengths(key, part):
    first, second = jax.random.split(jax.random.fold_in(key, 3))
    lengths = jax.random.randint(first, (NPROMPT,), PMOST // 8, PMOST + 1, dtype=jnp.int32)
    chosen = jax.random.randint(second, (), 0, NPROMPT, dtype=jnp.int32)
    return jnp.where(jnp.arange(NPROMPT, dtype=jnp.int32) == chosen, PMOST, lengths).astype(jnp.int32)


def draw_tail_lengths(key, part):
    first, second = jax.random.split(jax.random.fold_in(key, 5))
    lengths = jax.random.randint(first, (CONT,), TAIL_MIN, TAIL_MAX + 1, dtype=jnp.int32)
    chosen = jax.random.randint(second, (), 0, CONT, dtype=jnp.int32)
    return jnp.where(jnp.arange(CONT, dtype=jnp.int32) == chosen, TAIL_MAX, lengths).astype(jnp.int32)


def draw_prompt_of(key, part):
    order = jax.random.permutation(jax.random.fold_in(key, 7), CONT)
    return (order % NPROMPT).astype(jnp.int32)


def draw_page_table(key, part):
    order = jax.random.permutation(jax.random.fold_in(key, 9), 2 * CONT)
    return order.reshape(CONT, 2).astype(jnp.int32)


def place_ends(entries, own_key, smallest, top_value):
    dims = entries.shape
    index_at = [jax.random.randint(jax.random.fold_in(own_key, axis), (), 0, dims[axis]) for axis in range(len(dims))]
    entries = entries.at[tuple(index_at)].set(smallest)
    longest = dims.index(max(dims))
    index_at[longest] = (index_at[longest] + 1) % dims[longest]
    return entries.at[tuple(index_at)].set(top_value)


def spiked(result, stream_key, source, target, shards_of, factor):
    def block_of(dim):
        return (jnp.arange(result.shape[dim]) // (result.shape[dim] // shards_of)).reshape((-1,) + (1,) * (result.ndim - 1 - dim))

    first = jax.random.permutation(stream_key, shards_of)[block_of(target)]
    far = (block_of(target) + shards_of // 2) % shards_of
    return jnp.where((block_of(source) == first) | (block_of(source) == far), factor * result, result)


def steps_of(rng, extent, shards, least, high):
    loudness, own = 1.0, jax.random.fold_in(rng, 6)
    for dim, shards_of in shards:
        draws = jnp.exp(jax.random.uniform(jax.random.fold_in(own, dim), (shards_of,), jnp.float32, least / len(shards), high / len(shards)))
        loudness = loudness * jnp.repeat(draws, extent[dim] // shards_of).reshape([-1 if axis == dim else 1 for axis in range(len(extent))])
    return loudness


def rank_bounds(count, skew):
    portions = [(1 << 20) // math.isqrt(rank ** skew) + 1 for rank in range(1, count + 1)]
    deviation = 1 + sum(portions) // (1 << 30)
    return np.cumsum(np.array([max(1, weight // deviation) for weight in portions]))


def ranked_ids(key, extent, number_of, lean):
    table = rank_bounds(number_of, lean)
    ticket = jax.random.randint(jax.random.fold_in(key, 1), extent, 0, int(table[number_of - 1]))
    rank = jnp.searchsorted(jnp.asarray(table, jnp.int32), ticket, side="right")
    return jax.random.permutation(jax.random.fold_in(key, 2), number_of)[rank].astype(jnp.int32)


def normal_values(key, dims, width, bound, pieces=(), kind=jnp.bfloat16):
    factor_of = steps_of(key, dims, pieces, -0.22, 0.18) if pieces else 1.0
    values = jax.random.normal(key, dims, jnp.float32) * width * factor_of
    return jnp.minimum(jnp.maximum(values, -bound), bound).astype(kind)


def heavy_noise(rng, shape, scale, bound, shards, heavy, held_as=jnp.bfloat16):
    values = scale * jax.random.normal(rng, shape, jnp.float32)
    if shards:
        values = values * steps_of(rng, shape, shards, -0.22, 0.18)
    return jnp.clip(spiked(values, jax.random.fold_in(rng, 3), *heavy), -bound, bound).astype(held_as)


def setup_inputs(seed: int = 0) -> dict:
    arg_keys = jax.random.split(jax.random.key(seed), 18)
    token_ids = place_ends(ranked_ids(arg_keys[0], (CONT, 2), VOCAB, 2), jax.random.fold_in(arg_keys[0], 3), 0, VOCAB - 1).astype(jnp.int32)
    prompt_lengths = draw_prompt_lengths(jax.random.fold_in(arg_keys[17], 71), 0)
    tail_lengths = draw_tail_lengths(jax.random.fold_in(arg_keys[17], 71), 0)
    prompt_of = draw_prompt_of(jax.random.fold_in(arg_keys[17], 71), 0)
    page_table = draw_page_table(jax.random.fold_in(arg_keys[17], 71), 0)
    prompt_keys = draw_prompt_keys(jax.random.fold_in(arg_keys[17], 71), 0)
    prompt_values = normal_values(arg_keys[6], (CACHE, HEADS * HD), 2.0, 12.0, ((0, 64), (1, 8)))
    tail_keys = draw_tail_keys(jax.random.fold_in(arg_keys[17], 71), 0)
    tail_values = normal_values(arg_keys[8], (POOL * PAGE, HEADS * HD), 2.0, 12.0, ((0, 64), (1, 8)))
    norm_gain = jnp.clip(1.0 + 0.1 * jax.random.normal(arg_keys[9], (2, D), jnp.float32), 0.5, 1.5).astype(jnp.bfloat16)
    norm_bias = normal_values(arg_keys[10], (2, D), 0.3, 2.0, ((1, 64),))
    qkv_weight = normal_values(arg_keys[11], (D, 3, HEADS * HD), D ** -0.5, 0.0625, ((0, 64), (2, 8)))
    qkv_bias = normal_values(arg_keys[12], (3, HEADS * HD), 0.3, 2.0, ((1, 8),))
    out_weight = normal_values(arg_keys[13], (HEADS * HD, D), (HEADS * HD) ** -0.5, 0.078125, ((0, 8), (1, 64)))
    out_bias = normal_values(arg_keys[14], (D,), 0.1, 0.796875, ((0, 64),))
    embedding = heavy_noise(arg_keys[15], (VOCAB, D), 0.05, 0.3984375, ((0, 8), (1, 64)), (1, 0, 64, 4.0))
    score_weight = normal_values(arg_keys[16], (D,), D ** -0.5, 0.0625, ((0, 64),))
    return {"token_ids": token_ids, "prompt_lengths": prompt_lengths, "tail_lengths": tail_lengths, "prompt_of": prompt_of, "page_table": page_table, "prompt_keys": prompt_keys, "prompt_values": prompt_values, "tail_keys": tail_keys, "tail_values": tail_values, "norm_gain": norm_gain, "norm_bias": norm_bias, "qkv_weight": qkv_weight, "qkv_bias": qkv_bias, "out_weight": out_weight, "out_bias": out_bias, "embedding": embedding, "score_weight": score_weight}


epsilon = 1e-05
neg_fill = -1e+30

def normalize(values, gain, offset):
    average = lax.optimization_barrier(jnp.mean(values, axis=-1, keepdims=True))
    centered = values - average
    variance = lax.optimization_barrier(jnp.mean(centered * centered, axis=-1, keepdims=True))
    return centered * lax.rsqrt(variance + epsilon) * gain + offset

def reference(token_ids, prompt_lengths, tail_lengths, prompt_of, page_table, prompt_keys, prompt_values, tail_keys, tail_values, norm_gain, norm_bias, qkv_weight, qkv_bias, out_weight, out_bias, embedding, score_weight):
    flat_ids = token_ids.reshape(ROWS).astype(jnp.int32)
    embedded = jnp.take(embedding, flat_ids, axis=0)
    inputs = embedded.astype(jnp.float32)
    normed = normalize(inputs, norm_gain[0].astype(jnp.float32), norm_bias[0].astype(jnp.float32)).astype(jnp.bfloat16)
    qkv = jnp.dot(normed, qkv_weight.reshape(D, 3 * HEADS * HD), preferred_element_type=jnp.float32)
    qkv = qkv + qkv_bias.reshape(3 * HEADS * HD).astype(jnp.float32)
    qkv = qkv.astype(jnp.bfloat16).reshape(ROWS, 3, HEADS, HD)
    starts = jnp.cumsum(prompt_lengths) - prompt_lengths
    begin = jnp.take(starts, prompt_of, axis=0)
    finish = begin + jnp.take(prompt_lengths, prompt_of, axis=0)
    position = jnp.arange(CACHE, dtype=jnp.int32)
    prompt_mask = (position[None, :] >= begin[:, None]) & (position[None, :] < finish[:, None])
    prompt_mask = jnp.repeat(prompt_mask, 2, axis=0)
    tail_offsets = jnp.arange(2 * PAGE, dtype=jnp.int32)
    tail_mask = jnp.repeat(tail_offsets[None, :] < tail_lengths[:, None], 2, axis=0)
    row_token = jnp.arange(ROWS, dtype=jnp.int32) % 2
    self_mask = jnp.arange(2, dtype=jnp.int32)[None, :] <= row_token[:, None]
    mask_all = jnp.concatenate([prompt_mask, tail_mask, self_mask], axis=1)
    query_heads = qkv[:, 0].transpose(1, 0, 2)
    newkey_heads = qkv[:, 1].transpose(1, 0, 2)
    newvalue_heads = qkv[:, 2].transpose(1, 0, 2)
    key_heads = prompt_keys.reshape(CACHE, HEADS, HD).transpose(1, 0, 2)
    value_heads = prompt_values.reshape(CACHE, HEADS, HD).transpose(1, 0, 2)
    flat_pages = page_table.reshape(CONT * 2).astype(jnp.int32)
    tailkey_heads = jnp.take(tail_keys.reshape(POOL, PAGE, HEADS, HD), flat_pages, axis=0).reshape(CONT, 2 * PAGE, HEADS, HD).transpose(2, 0, 1, 3)
    tailvalue_heads = jnp.take(tail_values.reshape(POOL, PAGE, HEADS, HD), flat_pages, axis=0).reshape(CONT, 2 * PAGE, HEADS, HD).transpose(2, 0, 1, 3)
    score_scale = 1.0 / math.sqrt(HD)

    def one_head(items):
        query, key_new, value_new, keys_prompt, values_prompt, keys_tail, values_tail = items
        scores_prompt = jnp.dot(query, keys_prompt.T, preferred_element_type=jnp.float32)
        query_pairs = query.reshape(CONT, 2, HD).astype(jnp.float32)
        scores_tail = jnp.einsum('ctd,cjd->ctj', query_pairs, keys_tail.astype(jnp.float32)).reshape(ROWS, 2 * PAGE)
        scores_self = jnp.einsum('ctd,csd->cts', query_pairs, key_new.reshape(CONT, 2, HD).astype(jnp.float32)).reshape(ROWS, 2)
        scores = jnp.concatenate([scores_prompt, scores_tail, scores_self], axis=1) * score_scale
        scores = jnp.where(mask_all, scores, neg_fill)
        greatest = lax.optimization_barrier(jnp.max(scores, axis=1, keepdims=True))
        weights = jnp.where(mask_all, jnp.exp(scores - greatest), 0.0)
        totals = lax.optimization_barrier(jnp.sum(weights, axis=1))
        rounded = weights.astype(jnp.bfloat16)
        summed = jnp.dot(rounded[:, :CACHE], values_prompt, preferred_element_type=jnp.float32)
        tail_part = rounded[:, CACHE:CACHE + 2 * PAGE].reshape(CONT, 2, 2 * PAGE).astype(jnp.float32)
        summed = summed + jnp.einsum('ctj,cjd->ctd', tail_part, values_tail.astype(jnp.float32)).reshape(ROWS, HD)
        self_part = rounded[:, CACHE + 2 * PAGE:].reshape(CONT, 2, 2).astype(jnp.float32)
        summed = summed + jnp.einsum('cts,csd->ctd', self_part, value_new.reshape(CONT, 2, HD).astype(jnp.float32)).reshape(ROWS, HD)
        return (summed / totals[:, None]).astype(jnp.bfloat16)
    attended = lax.map(one_head, (query_heads, newkey_heads, newvalue_heads, key_heads, value_heads, tailkey_heads, tailvalue_heads))
    attended = attended.transpose(1, 0, 2).reshape(ROWS, HEADS * HD)
    hidden = inputs + jnp.dot(attended, out_weight, preferred_element_type=jnp.float32) + out_bias.astype(jnp.float32)
    hidden_norms = jnp.sqrt(lax.optimization_barrier(jnp.sum(hidden * hidden, axis=1)) / D)
    last_rows = hidden.reshape(CONT, 2, D)[:, 1]
    final = normalize(last_rows, norm_gain[1].astype(jnp.float32), norm_bias[1].astype(jnp.float32)).astype(jnp.bfloat16)
    score_values = jnp.dot(final, score_weight, preferred_element_type=jnp.float32)
    logits = jnp.dot(final, embedding.T, preferred_element_type=jnp.float32)
    top_logits = lax.optimization_barrier(jnp.max(logits, axis=1))
    return (hidden.astype(jnp.bfloat16), score_values, hidden_norms, top_logits)
```

```python
import math

import jax
import jax.numpy as jnp
from jax import lax
from jax.experimental import pallas as pl
from jax.experimental.pallas import tpu as pltpu
from jax.sharding import PartitionSpec as P

D = 7168
HD = 128
PAGE = 128
NX, NY, NC, NZ = 4, 8, 2, 8
CONT = 96
R = 256
DL = 112
HALF = 384
VL = 3200
HC = 48
WX = 896
EPS = 1e-05
NEG = -1e30
LEAST = -1e29
LOW = -3e38
SCALE = 1.0 / math.sqrt(HD)
BF = jnp.bfloat16
F32 = jnp.float32
HI = lax.Precision.HIGHEST
MESH = pl.DeviceIdType.MESH

NN = (((1,), (0,)), ((), ()))
NT = (((1,), (1,)), ((), ()))


def mm(a, b, dims=NN, precision=None):
    return lax.dot_general(a, b, dims, precision=precision, preferred_element_type=F32)


def iota(shape, axis):
    return lax.broadcasted_iota(jnp.int32, shape, axis)


def round_bf(v):
    return v.astype(BF).astype(F32)


def kernel(
    lens,
    tok,
    tails,
    prompt,
    pages,
    gain,
    offset,
    qkv_bias,
    out_bias,
    score_weight,
    pk_hbm,
    pv_hbm,
    tk_hbm,
    tv_hbm,
    w_hbm,
    wo_hbm,
    emb_hbm,
    hid_out,
    score_out,
    norm_out,
    top_out,
    pk,
    pv,
    tk,
    tv,
    w,
    wo,
    emb,
    bias,
    normed,
    gp,
    za_s,
    za_r,
    zi,
    st_z,
    st_c,
    st_y,
    qc_s,
    qc_r,
    q_f,
    qx_s,
    qx_r,
    qy_s,
    qy_r,
    qay,
    qac,
    kc_s,
    kc_r,
    kv_f,
    kx_s,
    kx_r,
    ky_s,
    ky_r,
    o_f,
    ml_f,
    oc_s,
    oc_r,
    ox_s,
    ox_r,
    oy_s,
    oy_r,
    aay,
    aac,
    hz_s,
    hz_r,
    hs_c,
    hs_y,
    hid,
    fin,
    nrm,
    lc_s,
    lc_r,
    l_f,
    lx_s,
    lx_r,
    ly_s,
    ly_r,
    sc_c,
    sc_y,
    mx_c,
    mx_y,
    mx_z,
    ssem,
    rsem,
    lsem,
):
    seq = lax.axis_index("seq")
    mz = lax.axis_index("mp")
    x = seq // 16
    y = (seq // 2) % 8
    c = seq % 2
    k = x * 2 + c
    oc = 1 - c

    def dev_c(d):
        return (x * 16 + y * 2 + (c + d) % 2, mz)

    def dev_x(d):
        return (((x + d) % NX) * 16 + y * 2 + c, mz)

    def dev_y(d):
        return (x * 16 + ((y + d) % NY) * 2 + c, mz)

    def dev_k(d):
        t = (k + d) % 8
        return ((t // 2) * 16 + y * 2 + t % 2, mz)

    def dev_z(d):
        return (seq, (mz + d) % NZ)

    waits = []

    def gather(s, buf, at, dev, n):
        for d in range(1, n):
            pltpu.make_async_remote_copy(
                src_ref=buf.at[at],
                dst_ref=buf.at[at],
                send_sem=ssem.at[s],
                recv_sem=rsem.at[s],
                device_id=dev(d),
                device_id_type=MESH,
            ).start()
        waits.append((s, buf.at[pl.ds(0, n - 1)]))

    def gathered(s, buf, n):
        part = buf.at[pl.ds(0, n - 1)]
        pltpu.make_async_copy(part, part, rsem.at[s]).wait()

    def scatter(s, src, dst, dev, at, n):
        for d in range(1, n):
            pltpu.make_async_remote_copy(
                src_ref=src.at[at(d)],
                dst_ref=dst.at[d - 1],
                send_sem=ssem.at[s],
                recv_sem=rsem.at[s],
                device_id=dev(d),
                device_id_type=MESH,
            ).start()
        waits.append((s, dst))

    def scattered(s, dst):
        pltpu.make_async_copy(dst, dst, rsem.at[s]).wait()

    def to_x(d):
        return (x + d) % NX

    def to_y(d):
        return (y + d) % NY

    def to_z(d):
        return (mz + d) % NZ

    def zero(d):
        return 0

    loads = [
        pltpu.make_async_copy(a, b, lsem.at[i])
        for i, (a, b) in enumerate(
            (
                (emb_hbm, emb),
                (w_hbm, w),
                (pk_hbm, pk),
                (tk_hbm, tk),
                (pv_hbm, pv),
                (tv_hbm, tv),
                (wo_hbm, wo),
            )
        )
    ]
    for load in loads:
        load.start()

    barrier = pltpu.get_barrier_semaphore()
    for dev in (dev_k, dev_y, dev_z):
        for d in range(1, 8):
            pl.semaphore_signal(barrier, inc=1, device_id=dev(d), device_id_type=MESH)

    row = iota((R, CONT), 0)
    slot = row % 8
    of_cont = ((row // 8) * 3 + slot // 2 == iota((R, CONT), 1)) & (slot < 6)
    i8 = iota((8, CONT), 0)
    facts = jnp.where(i8 == 0, prompt[...], 0)
    facts = jnp.where(i8 == 1, tails[...], facts)
    facts = jnp.where(i8 == 2, pages[0:1, :], facts)
    facts = jnp.where(i8 == 3, pages[1:2, :], facts)
    facts = jnp.where(i8 == 4, tok[0:1, :], facts)
    facts = jnp.where(i8 == 5, tok[1:2, :], facts)
    facts = mm(jnp.where(of_cont, 1.0, 0.0).astype(F32), facts.astype(F32), NT, HI)
    facts = (facts + 0.5).astype(jnp.int32)
    slot1 = iota((R, 1), 0) % 8
    real = slot1 < 6
    ids = jnp.where(slot1 % 2 == 0, facts[:, 4:5], facts[:, 5:6])
    ids = jnp.where(real, ids - mz * VL, -1)

    loads[0].wait()
    pick_chunk = 640

    def pick(i, total):
        at = pl.multiple_of(i * pick_chunk, pick_chunk)
        lane = iota((R, pick_chunk), 1) + at
        hot = jnp.where(lane == ids, 1.0, 0.0).astype(BF)
        return total + mm(hot, emb[:, pl.ds(at, pick_chunk)], NT)

    picked = lax.fori_loop(0, VL // pick_chunk, pick, jnp.zeros((R, DL), F32))
    wide = jnp.concatenate([picked, jnp.zeros((R, 128 - DL), F32)], axis=1)
    za_s[...] = wide.reshape(NZ, 32, 128).astype(BF)
    ones = jnp.ones((8, 128), F32)
    i128 = iota((8, 128), 0)
    squares = wide * wide
    stat = jnp.where(i128 == 0, mm(ones, wide[:128], NT, HI), 0.0)
    stat = jnp.where(i128 == 1, mm(ones, wide[128:], NT, HI), stat)
    stat = jnp.where(i128 == 2, mm(ones, squares[:128], NT, HI), stat)
    stat = jnp.where(i128 == 3, mm(ones, squares[128:], NT, HI), stat)
    st_z[mz] = stat

    pl.semaphore_wait(barrier, 21)
    gather(1, st_z, mz, dev_z, NZ)
    scatter(0, za_s, za_r, dev_z, to_z, NZ)

    gp[...] = jnp.zeros_like(gp)
    gp[0:2, :DL] = gain[...].astype(F32)
    gp[2:4, :DL] = offset[...].astype(F32)
    gp[4:5, :DL] = out_bias[...].astype(F32)
    gp[5:6, :DL] = score_weight[...].astype(F32)

    whose = facts[:, 0:1]
    begin = jnp.zeros((R, 1), jnp.int32)
    length = jnp.zeros((R, 1), jnp.int32)
    for j in range(6):
        begin = begin + jnp.where(whose > j, lens[j], 0)
        length = jnp.where(whose == j, lens[j], length)
    begin = begin - seq * 768
    finish = jnp.where(real, begin + length, begin)
    place = iota((R, 768), 1)
    bias[:, :768] = jnp.where((place >= begin) & (place < finish), 0.0, NEG).astype(F32)
    kept = jnp.where(real, facts[:, 1:2], 0)
    lane = iota((R, PAGE), 1)
    for j in range(3):
        page = seq * 3 + j
        held = jnp.where(facts[:, 2:3] == page, kept, 0)
        held = jnp.where(facts[:, 3:4] == page, kept - PAGE, held)
        bias[:, 768 + j * PAGE : 768 + (j + 1) * PAGE] = jnp.where(lane < held, 0.0, NEG).astype(F32)

    gathered(1, st_z, NZ)
    total = st_z[0]
    for i in range(1, 8):
        total = total + st_z[i]
    st_c[k] = total
    gather(2, st_c, k, dev_k, 8)

    scattered(0, za_r)
    own = za_s[mz].astype(F32)
    for i in range(7):
        own = own + za_r[i].astype(F32)
    zi[mz] = own.astype(BF)
    gather(4, zi, mz, dev_z, NZ)

    gathered(2, st_c, 8)
    total = st_c[0]
    for i in range(1, 8):
        total = total + st_c[i]
    st_y[y] = total
    gather(3, st_y, y, dev_y, NY)
    gathered(4, zi, NZ)
    loads[1].wait()
    gathered(3, st_y, NY)
    total = st_y[0]
    for i in range(1, 8):
        total = total + st_y[i]
    mean = total[0:2] * (1.0 / D)
    rstd = lax.rsqrt(total[2:4] * (1.0 / D) - mean * mean + EPS)
    eye = jnp.where(iota((128, 128), 0) == iota((128, 128), 1), 1.0, 0.0).astype(F32)
    for b in range(2):
        both = jnp.where(i128 == 0, mean[b : b + 1], jnp.where(i128 == 1, rstd[b : b + 1], 0.0))
        cols = mm(eye, both, NT, HI)
        part = zi[4 * b : 4 * b + 4].reshape(128, 128).astype(F32)
        part = (part - cols[:, 0:1]) * cols[:, 1:2] * gp[0:1, :] + gp[2:3, :]
        normed[b * 128 : (b + 1) * 128, :] = part.astype(BF)

    mine_at = pl.multiple_of(c * HALF, 128)
    other_at = pl.multiple_of(oc * HALF, 128)
    rows = normed[:, :DL]
    qc_s[0] = mm(rows, w[0, :, pl.ds(other_at, HALF)]).astype(BF)
    scatter(5, qc_s, qc_r, dev_c, zero, 2)
    q_f[...] = mm(rows, w[0, :, pl.ds(mine_at, HALF)])
    for j in range(2):
        kc_s[0, j] = mm(rows, w[1 + j, :, pl.ds(other_at, HALF)]).astype(BF)
    scattered(5, qc_r)
    full = q_f[...] + qc_r[0].astype(F32)
    q_f[...] = full
    qx_s[...] = full.reshape(NX, 64, HALF).astype(BF)
    scatter(6, qx_s, qx_r, dev_x, to_x, NX)
    scatter(10, kc_s, kc_r, dev_c, zero, 2)
    for j in range(2):
        kv_f[j] = mm(rows, w[1 + j, :, pl.ds(mine_at, HALF)])
    my_rows = pl.ds(pl.multiple_of(x * 64, 64), 64)
    scattered(6, qx_r)
    part = q_f[my_rows, :]
    for i in range(3):
        part = part + qx_r[i].astype(F32)
    qy_s[...] = part.reshape(NY, 8, HALF)
    scatter(7, qy_s, qy_r, dev_y, to_y, NY)
    scattered(10, kc_r)
    for j in range(2):
        full = kv_f[j] + kc_r[0, j].astype(F32)
        kv_f[j] = full
        for i in range(NX):
            kx_s[i, j] = full[i * 64 : (i + 1) * 64].astype(BF)
    scattered(7, qy_r)
    query = qy_s[y]
    for i in range(7):
        query = query + qy_r[i]
    query = round_bf(query + qkv_bias[0:1, pl.ds(mine_at, HALF)].astype(F32))
    qay[y] = query
    gather(8, qay, y, dev_y, NY)
    gathered(8, qay, NY)
    qac[k] = qay[...].reshape(64, HALF).astype(BF)
    gather(9, qac, k, dev_k, 8)
    for load in loads[2:6]:
        load.wait()
    gathered(9, qac, 8)
    scatter(11, kx_s, kx_r, dev_x, to_x, NX)

    lane_r = iota((R, 128), 1)

    def attend(half, which):
        ml_f[which] = jnp.zeros((R, 128), F32)

        def head(hh, carry):
            hl = pl.ds(pl.multiple_of(hh * HD, HD), HD)
            hg = pl.ds(pl.multiple_of(half * HALF + hh * HD, HD), HD)
            q = jnp.concatenate([qac[2 * i + half, :, hl] for i in range(NX)], axis=0)
            s1 = mm(q, pk[:, hg], NT) * SCALE + bias[:, :768]
            s2 = mm(q, tk[:, hg], NT) * SCALE + bias[:, 768:]
            m = jnp.maximum(jnp.max(s1, axis=1, keepdims=True), jnp.max(s2, axis=1, keepdims=True))
            m = jnp.maximum(m, LEAST)
            m1 = round_bf(m)
            m2 = round_bf(m - m1)
            base = m1 + m2
            e1 = jnp.exp(s1 - base)
            e2 = jnp.exp(s2 - base)
            l = jnp.sum(e1, axis=1, keepdims=True) + jnp.sum(e2, axis=1, keepdims=True)
            o_f[which, :, hl] = mm(e1.astype(BF), pv[:, hg]) + mm(e2.astype(BF), tv[:, hg])
            ml = ml_f[which]
            ml = jnp.where(lane_r == hh, base, ml)
            ml_f[which] = jnp.where(lane_r == 3 + hh, l, ml)
            return carry

        lax.fori_loop(0, 3, head, 0)

    def pack(ml, lanes):
        first = round_bf(ml)
        second = ml - first
        n = ml.shape[0]
        out = jnp.where(lanes < 6, first, 0.0)
        return jnp.where((lanes >= 64) & (lanes < 70), pltpu.roll(second, 64, 1), out)

    def unpack(t):
        return t + pltpu.roll(t, 64, 1)

    attend(oc, 0)
    oc_s[0, :, :HALF] = o_f[0].astype(BF)
    oc_s[0, :, HALF:] = pack(ml_f[0], lane_r).astype(BF)
    scatter(13, oc_s, oc_r, dev_c, zero, 2)

    scattered(11, kx_r)
    for j in range(2):
        part = kv_f[j, my_rows, :]
        for i in range(3):
            part = part + kx_r[i, j].astype(F32)
        for i in range(NY):
            ky_s[i, j] = part[i * 8 : (i + 1) * 8]
    scatter(12, ky_s, ky_r, dev_y, to_y, NY)
    attend(c, 1)

    def merge(parts, lanes, extra=None):
        greatest = parts[0][1]
        for _, ml in parts[1:]:
            greatest = jnp.maximum(greatest, ml)
        if extra is not None:
            greatest = jnp.maximum(greatest, extra)
        sums, totals = [None] * 3, None
        for o, ml in parts:
            f = jnp.exp(ml - greatest)
            t = pltpu.roll(f, 3, 1) * ml
            totals = t if totals is None else totals + t
            for h in range(3):
                term = o[:, h * HD : (h + 1) * HD] * f[:, h : h + 1]
                sums[h] = term if sums[h] is None else sums[h] + term
        return sums, jnp.where(lanes < 3, greatest, totals), greatest

    scattered(13, oc_r)
    sums, ml, _ = merge(
        [
            (o_f[1], jnp.where(lane_r < 6, ml_f[1], 0.0)),
            (
                oc_r[0, :, :HALF].astype(F32),
                jnp.where(lane_r < 6, unpack(oc_r[0, :, HALF:].astype(F32)), 0.0),
            ),
        ],
        lane_r,
    )
    packed = pack(ml, lane_r)
    for h in range(3):
        o_f[0, :, h * HD : (h + 1) * HD] = sums[h]
        ox_s[:, :, h * HD : (h + 1) * HD] = sums[h].reshape(NX, 64, HD).astype(BF)
    ml_f[0] = ml
    ox_s[:, :, HALF:] = packed.reshape(NX, 64, 128).astype(BF)
    scatter(14, ox_s, ox_r, dev_x, to_x, NX)
    lane_x = iota((64, 128), 1)
    scattered(14, ox_r)
    parts = [(o_f[0, my_rows, :], jnp.where(lane_x < 6, ml_f[0, my_rows, :], 0.0))]
    for i in range(3):
        parts.append(
            (
                ox_r[i, :, :HALF].astype(F32),
                jnp.where(lane_x < 6, unpack(ox_r[i, :, HALF:].astype(F32)), 0.0),
            )
        )
    sums, ml, _ = merge(parts, lane_x)
    for h in range(3):
        oy_s[:, :, h * HD : (h + 1) * HD] = sums[h].reshape(NY, 8, HD)
    oy_s[:, :, HALF:] = jnp.where(lane_x < 6, ml, 0.0).reshape(NY, 8, 128)
    scatter(15, oy_s, oy_r, dev_y, to_y, NY)

    scattered(12, ky_r)
    key = ky_s[y, 0]
    value = ky_s[y, 1]
    for i in range(7):
        key = key + ky_r[i, 0]
        value = value + ky_r[i, 1]
    key = round_bf(key + qkv_bias[1:2, pl.ds(mine_at, HALF)].astype(F32))
    value = round_bf(value + qkv_bias[2:3, pl.ds(mine_at, HALF)].astype(F32))
    lane_8 = iota((8, 128), 1)
    odd = i128 % 2 == 1
    key_before = pltpu.roll(key, 1, 0)
    value_before = pltpu.roll(value, 1, 0)
    same = jnp.full((8, 128), NEG, F32)
    before = jnp.full((8, 128), NEG, F32)
    for h in range(3):
        hs = slice(h * HD, (h + 1) * HD)
        a = jnp.sum(query[:, hs] * key[:, hs], axis=1, keepdims=True) * SCALE
        b = jnp.sum(query[:, hs] * key_before[:, hs], axis=1, keepdims=True) * SCALE
        same = jnp.where(lane_8 == h, a, same)
        before = jnp.where((lane_8 == h) & odd, b, before)

    scattered(15, oy_r)
    parts = [(oy_s[y, :, :HALF], oy_s[y, :, HALF:])]
    for i in range(7):
        parts.append((oy_r[i, :, :HALF], oy_r[i, :, HALF:]))
    sums, ml, greatest = merge(parts, lane_8, jnp.maximum(same, before))
    w_same = jnp.exp(same - greatest)
    w_before = jnp.exp(before - greatest)
    totals = pltpu.roll(ml, 125, 1) + w_same + w_before
    w_same = round_bf(w_same)
    w_before = round_bf(w_before)
    for h in range(3):
        hs = slice(h * HD, (h + 1) * HD)
        o = sums[h] + w_same[:, h : h + 1] * value[:, hs] + w_before[:, h : h + 1] * value_before[:, hs]
        aay[y, :, hs] = o / totals[:, h : h + 1]
    gather(16, aay, y, dev_y, NY)
    loads[6].wait()
    gathered(16, aay, NY)
    aac[k] = aay[...].reshape(64, HALF).astype(BF)
    gather(17, aac, k, dev_k, 8)
    gathered(17, aac, 8)
    out = jnp.zeros((R, DL), F32)
    for half in range(2):
        part = jnp.concatenate([aac[2 * i + half] for i in range(NX)], axis=0)
        out = out + mm(part, wo[:, half * HALF : (half + 1) * HALF], NT)
    out = jnp.concatenate([out, jnp.zeros((R, 128 - DL), F32)], axis=1)
    hz_s[...] = out.reshape(NZ, 32, 128).astype(BF)
    scatter(18, hz_s, hz_r, dev_z, to_z, NZ)
    scattered(18, hz_r)
    hidden = hz_s[mz].astype(F32)
    for i in range(7):
        hidden = hidden + hz_r[i].astype(F32)
    hidden = hidden + zi[mz].astype(F32) + gp[4:5, :]
    tall = jnp.concatenate([hidden, jnp.zeros((96, 128), F32)], axis=0)
    hs_c[k] = jnp.where(i128 == 0, mm(ones, tall, NT, HI), mm(ones, tall * tall, NT, HI))
    gather(19, hs_c, k, dev_k, 8)
    hid[mz] = hidden.astype(BF)
    gather(21, hid, mz, dev_z, NZ)
    gathered(19, hs_c, 8)
    total = hs_c[0]
    for i in range(1, 8):
        total = total + hs_c[i]
    hs_y[y] = total
    gather(20, hs_y, y, dev_y, NY)
    gathered(20, hs_y, NY)
    total = hs_y[0]
    for i in range(1, 8):
        total = total + hs_y[i]
    mean = total[0:1] * (1.0 / D)
    square = total[1:2] * (1.0 / D)
    rstd = lax.rsqrt(square - mean * mean + EPS)
    both = jnp.where(i128 == 0, mean, jnp.where(i128 == 1, rstd, 0.0))
    cols = mm(eye[:32], both, NT, HI)
    final = ((hidden - cols[:, 0:1]) * cols[:, 1:2] * gp[1:2, :] + gp[3:4, :]).astype(BF)
    i16 = iota((16, 32), 0)
    last = (iota((16, 32), 1) == 8 * (i16 // 3) + 2 * (i16 % 3) + 1) & (i16 < 12)
    fin[mz] = mm(jnp.where(last, 1.0, 0.0).astype(BF), final).astype(BF)
    gather(22, fin, mz, dev_z, NZ)
    nrm[mz] = jnp.where(i128 == 0, jnp.sqrt(square), 0.0)
    gather(23, nrm, mz, dev_z, NZ)
    gathered(22, fin, NZ)

    finals = fin[...].reshape(128, 128)

    def rows_of(n, start):
        cont = iota((n, 128), 0) + start
        hot = iota((n, 128), 1) == (cont // 12) * 16 + cont % 12
        return mm(jnp.where(hot & (cont < CONT), 1.0, 0.0).astype(BF), finals).astype(BF)

    lc_s[0] = mm(rows_of(HC, oc * HC)[:, :DL], emb[...]).astype(BF)
    scatter(24, lc_s, lc_r, dev_c, zero, 2)
    sc_c[k] = mm(jnp.broadcast_to(gp[5:6, :], (8, 128)).astype(BF), rows_of(128, 0), NT)
    gather(27, sc_c, k, dev_k, 8)
    l_f[...] = mm(rows_of(HC, c * HC)[:, :DL], emb[...])
    scattered(24, lc_r)
    full = l_f[...] + lc_r[0].astype(F32)
    l_f[...] = full
    for i, t in enumerate((0, 7, 14, 18)):
        lx_s[i] = full[:, t * 128 : t * 128 + WX].astype(BF)
    scatter(25, lx_s, lx_r, dev_x, to_x, NX)
    gathered(27, sc_c, 8)
    total = sc_c[0]
    for i in range(1, 8):
        total = total + sc_c[i]
    sc_y[y] = total
    gather(28, sc_y, y, dev_y, NY)

    gathered(21, hid, NZ)
    out_row = iota((192, R), 0)
    back = iota((192, R), 1) == (out_row // 6) * 8 + out_row % 6
    states = mm(jnp.where(back, 1.0, 0.0).astype(BF), hid[...].reshape(R, 128))
    hid_out[...] = states[:, :DL].astype(BF)
    gathered(23, nrm, NZ)
    norms = jnp.zeros((8, 192), F32)
    for i in range(NZ):
        col = iota((128, 192), 1)
        at = (col // 6) * 8 + col % 6 - i * 32
        norms = norms + mm(nrm[i], jnp.where(iota((128, 192), 0) == at, 1.0, 0.0).astype(F32), NN, HI)
    norm_out[...] = norms[0:1]

    scattered(25, lx_r)
    at = pl.multiple_of((7 * x - 3 * (x // 3)) * 128, 128)
    part = l_f[:, pl.ds(at, WX)]
    for i in range(3):
        part = part + lx_r[i].astype(F32)
    for i in range(7):
        ly_s[i] = part[:, i * 128 : (i + 1) * 128].astype(BF)

    def word_tile(d):
        t = (y + d) % NY
        return t - t // 7

    scatter(26, ly_s, ly_r, dev_y, word_tile, NY)
    gathered(28, sc_y, NY)
    total = sc_y[0]
    for i in range(1, 8):
        total = total + sc_y[i]
    score_out[...] = total[0:1, :CONT]
    scattered(26, ly_r)
    logits = ly_s[word_tile(0)].astype(F32)
    for i in range(7):
        logits = logits + ly_r[i].astype(F32)
    top = jnp.max(logits, axis=1, keepdims=True)
    lane_h = iota((HC, 128), 1) - c * HC
    row_h = iota((HC, 128), 0)
    top = jnp.sum(jnp.where(lane_h == row_h, top, 0.0), axis=0, keepdims=True)
    lane_1 = lane_8 - c * HC
    best = jnp.where((lane_1 >= 0) & (lane_1 < HC), top, LOW)
    for s, buf, at, dev in ((29, mx_c, k, dev_k), (30, mx_y, y, dev_y), (31, mx_z, mz, dev_z)):
        buf[at] = best
        gather(s, buf, at, dev, 8)
        gathered(s, buf, 8)
        best = buf[0]
        for i in range(1, 8):
            best = jnp.maximum(best, buf[i])
    top_out[...] = best[0:1, :CONT]

    for s, part in waits:
        pltpu.make_async_copy(part, part, ssem.at[s]).wait()


def per_device(
    token_ids,
    prompt_lengths,
    tail_lengths,
    prompt_of,
    page_table,
    prompt_keys,
    prompt_values,
    tail_keys,
    tail_values,
    norm_gain,
    norm_bias,
    qkv_weight,
    qkv_bias,
    out_weight,
    out_bias,
    embedding,
    score_weight,
):
    vm = pl.BlockSpec(memory_space=pltpu.VMEM)
    hbm = pl.BlockSpec(memory_space=pl.ANY)
    sm = pl.BlockSpec(memory_space=pltpu.SMEM)

    def b(*shape):
        return pltpu.VMEM(shape, BF)

    def f(*shape):
        return pltpu.VMEM(shape, F32)

    scratch = [
        b(768, 768),
        b(768, 768),
        b(384, 768),
        b(384, 768),
        b(3, DL, 768),
        b(DL, 768),
        b(DL, VL),
        f(R, 1152),
        b(R, 128),
        f(8, 128),
        b(8, 32, 128),
        b(7, 32, 128),
        b(8, 32, 128),
        f(8, 8, 128),
        f(8, 8, 128),
        f(8, 8, 128),
        b(1, R, HALF),
        b(1, R, HALF),
        f(R, HALF),
        b(NX, 64, HALF),
        b(3, 64, HALF),
        f(NY, 8, HALF),
        f(7, 8, HALF),
        f(NY, 8, HALF),
        b(8, 64, HALF),
        b(1, 2, R, HALF),
        b(1, 2, R, HALF),
        f(2, R, HALF),
        b(NX, 2, 64, HALF),
        b(3, 2, 64, HALF),
        f(NY, 2, 8, HALF),
        f(7, 2, 8, HALF),
        f(2, R, HALF),
        f(2, R, 128),
        b(1, R, 512),
        b(1, R, 512),
        b(NX, 64, 512),
        b(3, 64, 512),
        f(NY, 8, 512),
        f(7, 8, 512),
        f(NY, 8, HALF),
        b(8, 64, HALF),
        b(8, 32, 128),
        b(7, 32, 128),
        f(8, 8, 128),
        f(8, 8, 128),
        b(8, 32, 128),
        b(8, 16, 128),
        f(8, 8, 128),
        b(1, HC, VL),
        b(1, HC, VL),
        f(HC, VL),
        b(NX, HC, WX),
        b(3, HC, WX),
        b(7, HC, 128),
        b(7, HC, 128),
        f(8, 8, 128),
        f(8, 8, 128),
        f(8, 8, 128),
        f(8, 8, 128),
        f(8, 8, 128),
        pltpu.SemaphoreType.DMA((32,)),
        pltpu.SemaphoreType.DMA((32,)),
        pltpu.SemaphoreType.DMA((7,)),
    ]
    hidden, score, norms, top = pl.pallas_call(
        kernel,
        out_shape=(
            jax.ShapeDtypeStruct((192, DL), BF),
            jax.ShapeDtypeStruct((1, CONT), F32),
            jax.ShapeDtypeStruct((1, 192), F32),
            jax.ShapeDtypeStruct((1, CONT), F32),
        ),
        in_specs=[sm] + [vm] * 9 + [hbm] * 7,
        out_specs=(vm, vm, vm, vm),
        scratch_shapes=scratch,
        compiler_params=pltpu.CompilerParams(
            collective_id=0, has_side_effects=True, vmem_limit_bytes=40 * 2**20
        ),
    )(
        prompt_lengths,
        token_ids.T,
        tail_lengths.reshape(1, CONT),
        prompt_of.reshape(1, CONT),
        page_table.T,
        norm_gain,
        norm_bias,
        qkv_bias,
        out_bias.reshape(1, DL),
        score_weight.reshape(1, DL),
        prompt_keys,
        prompt_values,
        tail_keys,
        tail_values,
        qkv_weight.transpose(1, 0, 2),
        out_weight.T,
        embedding.T,
    )
    return hidden, score.reshape(CONT), norms.reshape(192), top.reshape(CONT)


def solution(mesh):
    return jax.shard_map(
        per_device,
        mesh=mesh,
        in_specs=(
            P(),
            P(),
            P(),
            P(),
            P(),
            P("seq", "mp"),
            P("seq", "mp"),
            P("seq", "mp"),
            P("seq", "mp"),
            P(None, "seq"),
            P(None, "seq"),
            P("seq", None, "mp"),
            P(None, "mp"),
            P("mp", "seq"),
            P("seq"),
            P("mp", "seq"),
            P("seq"),
        ),
        out_specs=(P(None, "seq"), P(), P(), P()),
        check_vma=False,
    )
```

```python
import math

import jax
import jax.numpy as jnp
from jax import lax
from jax.experimental import pallas as pl
from jax.experimental.pallas import tpu as pltpu
from jax.sharding import PartitionSpec as P

D = 7168
HD = 128
PAGE = 128
NX, NY, NC, NZ = 4, 8, 2, 8
CONT = 96
R = 256
DL = 112
HALF = 384
VL = 3200
HC = 48
TILES = 25
PLANE = NX * NY
NP = NC * NZ
EPS = 1e-05
NEG = -1e30
LEAST = -1e29
LOW = -3e38
SCALE = 1.0 / math.sqrt(HD)
BF = jnp.bfloat16
F32 = jnp.float32
MESH = pl.DeviceIdType.MESH

NN = (((1,), (0,)), ((), ()))
NT = (((1,), (1,)), ((), ()))


def mm(a, b, dims=NN):
    return lax.dot_general(a, b, dims, preferred_element_type=F32)


def iota(shape, axis):
    return lax.broadcasted_iota(jnp.int32, shape, axis)


def to_row(col):
    n = col.shape[0]
    return jnp.sum(jnp.where(iota((n, 128), 0) == iota((n, 128), 1), col, 0.0), axis=0, keepdims=True)


def to_col(row, n):
    return jnp.sum(jnp.where(iota((n, 128), 0) == iota((n, 128), 1), row, 0.0), axis=1, keepdims=True)


def round_bf(v):
    return v.astype(BF).astype(F32)


def kernel(
    lens_hbm,
    tok_hbm,
    tails_hbm,
    prompt_hbm,
    pages_hbm,
    gain_hbm,
    offset_hbm,
    qkv_bias_hbm,
    out_bias_hbm,
    score_weight_hbm,
    pk_hbm,
    pv_hbm,
    tk_hbm,
    tv_hbm,
    w_hbm,
    wo_hbm,
    emb_hbm,
    hid_out,
    score_out,
    norm_out,
    top_out,
    lens,
    tok,
    tails,
    prompt,
    pages,
    gain,
    offset,
    qkv_bias,
    out_bias,
    score_weight,
    pk,
    pv,
    tk,
    tv,
    w,
    wo,
    emb,
    bias,
    normed,
    gp,
    za_s,
    za_r,
    zi,
    gp_o,
    w_o,
    emb_o,
    st_p,
    st_z,
    q_f,
    qp_s,
    qp_r,
    qap,
    qac,
    kv_f,
    kp_s,
    kp_r,
    o_f,
    ml_f,
    oc_s,
    oc_r,
    op_s,
    op_r,
    aap,
    aac,
    hz_s,
    hz_r,
    hs_c,
    hs_p,
    hid,
    fin,
    nrm,
    l_f,
    lp_s,
    lp_r,
    mx_p,
    mx_z,
    ssem,
    rsem,
    lsem,
):
    seq = lax.axis_index("seq")
    mz = lax.axis_index("mp")
    x = seq // 16
    y = (seq // 2) % 8
    c = seq % 2
    p = x * NY + y
    oc = 1 - c
    pair = mz * NC + c
    pair_o = mz * NC + oc

    def dev_c(d):
        return (x * 16 + y * 2 + (c + d) % 2, mz)

    def far(v, n, t):
        return lax.rem(v + n // 2 + ((t + 1) // 2) * (1 - 2 * (t % 2)), n)

    def chips(visit):
        def along(i, carry):
            tx = lax.rem(x + 2 + lax.div(i + 1, 2) * (1 - 2 * lax.rem(i, 2)), NX)
            for t in range(NY - 1):
                visit(i * 8 + t, tx, far(y, NY, t))
            return carry

        lax.fori_loop(0, NX, along, 0)
        for i in range(NX - 1):
            visit(i * 8 + NY - 1, far(x, NX, i), y)

    def dev_chip(tx, ty):
        return (tx * 16 + ty * 2 + c, mz)

    def dev_pair(d):
        t = (pair + d) % NP
        return (x * 16 + y * 2 + t % NC, t // NC)

    def dev_z(d):
        return (seq, (mz + d) % NZ)

    waits = []

    def gather(s, buf, at, dev, n):
        for d in range(1, n):
            pltpu.make_async_remote_copy(
                src_ref=buf.at[at],
                dst_ref=buf.at[at],
                send_sem=ssem.at[s],
                recv_sem=rsem.at[s],
                device_id=dev(d),
                device_id_type=MESH,
            ).start()
        waits.append((s, buf.at[pl.ds(0, n - 1)]))

    def gathered(s, buf, n):
        part = buf.at[pl.ds(0, n - 1)]
        pltpu.make_async_copy(part, part, rsem.at[s]).wait()

    def scatter(s, src, dst, dev, at, n):
        for d in range(1, n):
            pltpu.make_async_remote_copy(
                src_ref=src.at[at(d)],
                dst_ref=dst.at[d - 1],
                send_sem=ssem.at[s],
                recv_sem=rsem.at[s],
                device_id=dev(d),
                device_id_type=MESH,
            ).start()
        waits.append((s, dst))

    def scattered(s, dst):
        pltpu.make_async_copy(dst, dst, rsem.at[s]).wait()

    def gather_p(s, buf):
        def send(j, tx, ty):
            pltpu.make_async_remote_copy(
                src_ref=buf.at[p],
                dst_ref=buf.at[p],
                send_sem=ssem.at[s],
                recv_sem=rsem.at[s],
                device_id=dev_chip(tx, ty),
                device_id_type=MESH,
            ).start()

        chips(send)
        waits.append((s, buf.at[pl.ds(0, PLANE - 1)]))

    def scatter_p(s, src, dst, at):
        def send(j, tx, ty):
            pltpu.make_async_remote_copy(
                src_ref=src.at[at(tx * NY + ty)],
                dst_ref=dst.at[j],
                send_sem=ssem.at[s],
                recv_sem=rsem.at[s],
                device_id=dev_chip(tx, ty),
                device_id_type=MESH,
            ).start()

        chips(send)
        waits.append((s, dst))

    def same_chip(t):
        return t

    def to_z(d):
        return (mz + d) % NZ

    def zero(d):
        return 0

    barrier = pltpu.get_barrier_semaphore()

    def greet(j, tx, ty):
        pl.semaphore_signal(barrier, inc=1, device_id=dev_chip(tx, ty), device_id_type=MESH)

    chips(greet)
    for d in range(1, NP):
        pl.semaphore_signal(barrier, inc=1, device_id=dev_pair(d), device_id_type=MESH)

    loads = [
        pltpu.make_async_copy(a, b, lsem.at[i])
        for i, (a, b) in enumerate(
            (
                (lens_hbm, lens),
                (tok_hbm, tok),
                (tails_hbm, tails),
                (prompt_hbm, prompt),
                (pages_hbm, pages),
                (gain_hbm, gain),
                (offset_hbm, offset),
                (qkv_bias_hbm, qkv_bias),
                (out_bias_hbm, out_bias),
                (score_weight_hbm, score_weight),
                (emb_hbm, emb),
                (w_hbm, w),
                (pk_hbm, pk),
                (tk_hbm, tk),
                (pv_hbm, pv),
                (tv_hbm, tv),
                (wo_hbm, wo),
            )
        )
    ]
    for load in loads:
        load.start()

    for load in loads[:10]:
        load.wait()
    row = iota((R, CONT), 0)
    slot = row % 8
    of_cont = ((row // 8) * 3 + slot // 2 == iota((R, CONT), 1)) & (slot < 6)
    slot1 = iota((R, 1), 0) % 8
    real = slot1 < 6

    def of_row(v):
        v = jnp.sum(jnp.where(of_cont, v.astype(F32), 0.0), axis=1, keepdims=True)
        return (v + 0.5).astype(jnp.int32)

    ids = of_row(jnp.where(slot % 2 == 0, tok[0:1, :], tok[1:2, :]))
    ids = jnp.where(real, ids - mz * VL, -1)

    loads[10].wait()
    pick_chunk = 640

    def pick(i, total):
        at = pl.multiple_of(i * pick_chunk, pick_chunk)
        lane = iota((R, pick_chunk), 1) + at
        hot = jnp.where(lane == ids, 1.0, 0.0).astype(BF)
        return total + mm(hot, emb[:, pl.ds(at, pick_chunk)], NT)

    picked = lax.fori_loop(0, VL // pick_chunk, pick, jnp.zeros((R, DL), F32))
    wide = jnp.concatenate([picked, jnp.zeros((R, 128 - DL), F32)], axis=1)
    za_s[...] = wide.reshape(NZ, 32, 128).astype(BF)
    squares = jnp.sum(wide * wide, axis=1, keepdims=True)
    plain = jnp.sum(wide, axis=1, keepdims=True)
    for b in range(2):
        st_p[p, b : b + 1] = to_row(plain[b * 128 : (b + 1) * 128])
        st_p[p, 2 + b : 3 + b] = to_row(squares[b * 128 : (b + 1) * 128])

    pl.semaphore_wait(barrier, PLANE - 1 + NP - 1)
    scatter(0, za_s, za_r, dev_z, to_z, NZ)
    gather_p(2, st_p)

    gp[...] = jnp.zeros_like(gp)
    gp[0:2, :DL] = gain[...].astype(F32)
    gp[2:4, :DL] = offset[...].astype(F32)
    gp[4:5, :DL] = out_bias[...].astype(F32)
    gp[5:6, :DL] = score_weight[...].astype(F32)

    mine_at = pl.multiple_of(c * HALF, 128)
    other_at = pl.multiple_of(oc * HALF, 128)
    loads[11].wait()

    def lend(s, src, dst):
        pltpu.make_async_remote_copy(
            src_ref=src,
            dst_ref=dst,
            send_sem=ssem.at[s],
            recv_sem=rsem.at[s],
            device_id=dev_c(1),
            device_id_type=MESH,
        ).start()
        waits.append((s, dst))

    lend(7, gp, gp_o)
    lend(5, w.at[:, :, pl.ds(other_at, HALF)], w_o)

    whose = of_row(prompt[...])
    begin = jnp.zeros((R, 1), jnp.int32)
    length = jnp.zeros((R, 1), jnp.int32)
    for j in range(6):
        begin = begin + jnp.where(whose > j, lens[0:1, j : j + 1], 0)
        length = jnp.where(whose == j, lens[0:1, j : j + 1], length)
    begin = begin - seq * 768
    finish = jnp.where(real, begin + length, begin)
    place = iota((R, 768), 1)
    bias[:, :768] = jnp.where((place >= begin) & (place < finish), 0.0, NEG).astype(F32)
    kept = jnp.where(real, of_row(tails[...]), 0)
    page0 = of_row(pages[0:1, :])
    page1 = of_row(pages[1:2, :])
    lane = iota((R, PAGE), 1)
    for j in range(3):
        page = seq * 3 + j
        held = jnp.where(page0 == page, kept, 0)
        held = jnp.where(page1 == page, kept - PAGE, held)
        bias[:, 768 + j * PAGE : 768 + (j + 1) * PAGE] = jnp.where(lane < held, 0.0, NEG).astype(F32)

    scattered(0, za_r)
    own = za_s[mz].astype(F32)
    for i in range(7):
        own = own + za_r[i].astype(F32)
    zi[pair] = own.astype(BF)
    gather(4, zi, pair, dev_pair, NP)
    gathered(2, st_p, PLANE)
    st_z[pair] = jnp.sum(st_p[...], axis=0)
    gather(3, st_z, pair, dev_pair, NP)
    scattered(7, gp_o)
    scattered(5, w_o)
    gathered(4, zi, NP)
    gathered(3, st_z, NP)
    total = jnp.sum(st_z[...], axis=0)
    mean = total[0:2] * (1.0 / D)
    rstd = lax.rsqrt(total[2:4] * (1.0 / D) - mean * mean + EPS)
    for b in range(2):
        mean_col = to_col(mean[b : b + 1], 128)
        rstd_col = to_col(rstd[b : b + 1], 128)
        for o, core, g in ((0, c, gp), (1, oc, gp_o)):
            part = jnp.concatenate([zi[NC * (4 * b + i) + core] for i in range(4)], axis=0)
            part = (part.astype(F32) - mean_col) * rstd_col
            normed[o, b * 128 : (b + 1) * 128, :] = (part * g[0:1, :] + g[2:3, :]).astype(BF)

    rows = normed[0, :, :DL]
    rows_o = normed[1, :, :DL]
    full = mm(rows, w[0, :, pl.ds(mine_at, HALF)]) + mm(rows_o, w_o[0])
    q_f[...] = full
    qp_s[...] = full.reshape(PLANE, 8, HALF).astype(BF)
    scatter_p(6, qp_s, qp_r, same_chip)
    lend(24, emb, emb_o)
    for j in range(2):
        full = mm(rows, w[1 + j, :, pl.ds(mine_at, HALF)]) + mm(rows_o, w_o[1 + j])
        kv_f[j] = full
        kp_s[:, j] = full.reshape(PLANE, 8, HALF).astype(BF)
    my_rows = pl.ds(pl.multiple_of(p * 8, 8), 8)
    scattered(6, qp_r)
    query = q_f[my_rows, :] + jnp.sum(qp_r[...].astype(F32), axis=0)
    query = round_bf(query + qkv_bias[0:1, pl.ds(mine_at, HALF)].astype(F32))
    qap[p] = query.astype(BF)
    gather_p(8, qap)
    scatter_p(11, kp_s, kp_r, same_chip)
    for load in loads[12:16]:
        load.wait()
    ml_f[...] = jnp.zeros_like(ml_f)
    gathered(8, qap, PLANE)
    qac[c] = qap[...]
    gather(9, qac, c, dev_c, NC)

    lane_r = iota((R, 128), 1)

    def attend(half, which, low, high):
        def head(hh, carry):
            hl = pl.ds(pl.multiple_of(hh * HD, HD), HD)
            hg = pl.ds(pl.multiple_of(half * HALF + hh * HD, HD), HD)
            q = qac[half, :, :, hl].astype(F32).reshape(R, HD).astype(BF)
            s1 = mm(q, pk[:, hg], NT) * SCALE + bias[:, :768]
            s2 = mm(q, tk[:, hg], NT) * SCALE + bias[:, 768:]
            m = jnp.maximum(jnp.max(s1, axis=1, keepdims=True), jnp.max(s2, axis=1, keepdims=True))
            m = jnp.maximum(m, LEAST)
            m1 = round_bf(m)
            m2 = round_bf(m - m1)
            base = m1 + m2
            e1 = jnp.exp(s1 - base)
            e2 = jnp.exp(s2 - base)
            l = jnp.sum(e1, axis=1, keepdims=True) + jnp.sum(e2, axis=1, keepdims=True)
            o_f[which, :, hl] = mm(e1.astype(BF), pv[:, hg]) + mm(e2.astype(BF), tv[:, hg])
            ml = ml_f[which]
            ml = jnp.where(lane_r == hh, base, ml)
            ml_f[which] = jnp.where(lane_r == 3 + hh, l, ml)
            return carry

        lax.fori_loop(low, high, head, 0)

    def pack(ml, lanes):
        first = round_bf(ml)
        second = ml - first
        n = ml.shape[0]
        out = jnp.where(lanes < 6, first, 0.0)
        return jnp.where((lanes >= 64) & (lanes < 70), pltpu.roll(second, 64, 1), out)

    def unpack(t):
        return t + pltpu.roll(t, 64, 1)

    attend(c, 1, 0, 1)
    gathered(9, qac, NC)
    attend(oc, 0, 0, 3)
    oc_s[0, :, :HALF] = o_f[0].astype(BF)
    oc_s[0, :, HALF:] = pack(ml_f[0], lane_r).astype(BF)
    scatter(13, oc_s, oc_r, dev_c, zero, 2)

    attend(c, 1, 1, 3)

    def merge(parts, lanes):
        greatest = parts[0][1]
        for _, ml in parts[1:]:
            greatest = jnp.maximum(greatest, ml)
        sums, totals = [None] * 3, None
        for o, ml in parts:
            f = jnp.exp(ml - greatest)
            t = pltpu.roll(f, 3, 1) * ml
            totals = t if totals is None else totals + t
            for h in range(3):
                term = o[:, h * HD : (h + 1) * HD] * f[:, h : h + 1]
                sums[h] = term if sums[h] is None else sums[h] + term
        return sums, jnp.where(lanes < 3, greatest, totals)

    scattered(13, oc_r)
    sums, ml = merge(
        [
            (o_f[1], jnp.where(lane_r < 6, ml_f[1], 0.0)),
            (
                oc_r[0, :, :HALF].astype(F32),
                jnp.where(lane_r < 6, unpack(oc_r[0, :, HALF:].astype(F32)), 0.0),
            ),
        ],
        lane_r,
    )
    packed = pack(ml, lane_r)
    for h in range(3):
        o_f[0, :, h * HD : (h + 1) * HD] = sums[h]
        op_s[:, :, h * HD : (h + 1) * HD] = sums[h].reshape(PLANE, 8, HD).astype(BF)
    ml_f[0] = ml
    op_s[:, :, HALF:] = packed.reshape(PLANE, 8, 128).astype(BF)
    scatter_p(14, op_s, op_r, same_chip)

    scattered(11, kp_r)
    key = kv_f[0, my_rows, :] + jnp.sum(kp_r[:, 0].astype(F32), axis=0)
    value = kv_f[1, my_rows, :] + jnp.sum(kp_r[:, 1].astype(F32), axis=0)
    key = round_bf(key + qkv_bias[1:2, pl.ds(mine_at, HALF)].astype(F32))
    value = round_bf(value + qkv_bias[2:3, pl.ds(mine_at, HALF)].astype(F32))
    lane_8 = iota((8, 128), 1)
    odd = iota((8, 128), 0) % 2 == 1
    key_before = pltpu.roll(key, 1, 0)
    value_before = pltpu.roll(value, 1, 0)
    same = jnp.full((8, 128), NEG, F32)
    before = jnp.full((8, 128), NEG, F32)
    for h in range(3):
        hs = slice(h * HD, (h + 1) * HD)
        a = jnp.sum(query[:, hs] * key[:, hs], axis=1, keepdims=True) * SCALE
        b = jnp.sum(query[:, hs] * key_before[:, hs], axis=1, keepdims=True) * SCALE
        same = jnp.where(lane_8 == h, a, same)
        before = jnp.where((lane_8 == h) & odd, b, before)

    mine = jnp.where(lane_8 < 6, ml_f[0, my_rows, :], 0.0)
    scattered(14, op_r)
    n31 = (PLANE - 1) * 8
    mls = unpack(op_r[:, :, HALF:].astype(F32).reshape(n31, 128))
    mls = jnp.where(iota((n31, 128), 1) < 6, mls, 0.0)
    ml3 = mls.reshape(PLANE - 1, 8, 128)
    greatest = jnp.maximum(jnp.maximum(jnp.max(ml3, axis=0), mine), jnp.maximum(same, before))
    f3 = jnp.exp(ml3 - greatest[None])
    f = jnp.exp(mine - greatest)
    t3 = (pltpu.roll(f3.reshape(n31, 128), 3, 1) * mls).reshape(PLANE - 1, 8, 128)
    ml = jnp.sum(t3, axis=0) + pltpu.roll(f, 3, 1) * mine
    sums = []
    for h in range(3):
        hs = slice(h * HD, (h + 1) * HD)
        o = jnp.sum(op_r[:, :, hs].astype(F32) * f3[:, :, h : h + 1], axis=0)
        sums.append(o + o_f[0, my_rows, hs] * f[:, h : h + 1])
    w_same = jnp.exp(same - greatest)
    w_before = jnp.exp(before - greatest)
    totals = pltpu.roll(ml, 125, 1) + w_same + w_before
    w_same = round_bf(w_same)
    w_before = round_bf(w_before)
    for h in range(3):
        hs = slice(h * HD, (h + 1) * HD)
        o = sums[h] + w_same[:, h : h + 1] * value[:, hs] + w_before[:, h : h + 1] * value_before[:, hs]
        aap[p, :, hs] = (o / totals[:, h : h + 1]).astype(BF)
    gather_p(16, aap)
    loads[16].wait()
    gathered(16, aap, PLANE)
    aac[c] = aap[...]
    gather(17, aac, c, dev_c, NC)
    gathered(17, aac, NC)
    out = jnp.zeros((R, DL), F32)
    for half in range(2):
        part = aac[half].astype(F32).reshape(R, HALF).astype(BF)
        out = out + mm(part, wo[:, half * HALF : (half + 1) * HALF], NT)
    out = jnp.concatenate([out, jnp.zeros((R, 128 - DL), F32)], axis=1)
    hz_s[...] = out.reshape(NZ, 32, 128).astype(BF)
    scatter(18, hz_s, hz_r, dev_z, to_z, NZ)
    scattered(18, hz_r)
    hidden = hz_s[mz].astype(F32)
    for i in range(7):
        hidden = hidden + hz_r[i].astype(F32)
    hidden = hidden + zi[pair].astype(F32) + gp[4:5, :]
    hs_c[c, 0:1] = to_row(jnp.sum(hidden, axis=1, keepdims=True))
    hs_c[c, 1:2] = to_row(jnp.sum(hidden * hidden, axis=1, keepdims=True))
    gather(19, hs_c, c, dev_c, NC)
    hid[mz] = hidden.astype(BF)
    gathered(19, hs_c, NC)
    hs_p[p] = hs_c[0] + hs_c[1]
    gather_p(20, hs_p)
    gathered(20, hs_p, PLANE)
    total = jnp.sum(hs_p[...], axis=0)
    mean = total[0:1] * (1.0 / D)
    square = total[1:2] * (1.0 / D)
    rstd = lax.rsqrt(square - mean * mean + EPS)
    final = (hidden - to_col(mean, 32)) * to_col(rstd, 32)
    final = (final * gp[1:2, :] + gp[3:4, :]).astype(BF)
    i16 = iota((16, 32), 0)
    last = (iota((16, 32), 1) == 8 * (i16 // 3) + 2 * (i16 % 3) + 1) & (i16 < 12)
    fin[pair] = mm(jnp.where(last, 1.0, 0.0).astype(BF), final).astype(BF)
    gather(22, fin, pair, dev_pair, NP)
    gather(21, hid, mz, dev_z, NZ)
    nrm[mz] = jnp.sqrt(square)
    gather(23, nrm, mz, dev_z, NZ)
    scattered(24, emb_o)
    gathered(22, fin, NP)

    finals = jnp.concatenate([fin[NC * i + c] for i in range(NZ)], axis=0)
    finals_o = jnp.concatenate([fin[NC * i + oc] for i in range(NZ)], axis=0)

    def rows_of(n, start, v):
        cont = iota((n, 128), 0) + start
        hot = iota((n, 128), 1) == (cont // 12) * 16 + cont % 12
        return mm(jnp.where(hot & (cont < CONT), 1.0, 0.0).astype(BF), v).astype(BF)

    full = mm(rows_of(HC, c * HC, finals)[:, :DL], emb[...])
    full = full + mm(rows_of(HC, c * HC, finals_o)[:, :DL], emb_o[...])
    l_f[...] = full
    for t in range(TILES):
        lp_s[t] = full[:, t * 128 : (t + 1) * 128].astype(BF)

    def send_words(j, tx, ty):
        t = tx * NY + ty

        @pl.when(t < TILES)
        def _():
            pltpu.make_async_remote_copy(
                src_ref=lp_s.at[t],
                dst_ref=lp_r.at[j],
                send_sem=ssem.at[25],
                recv_sem=rsem.at[25],
                device_id=dev_chip(tx, ty),
                device_id_type=MESH,
            ).start()

    chips(send_words)
    score = mm(jnp.broadcast_to(gp[5:6, :], (8, 128)).astype(BF), rows_of(128, 0, finals), NT)
    mx_p[p, 1:2] = score[0:1]
    gathered(21, hid, NZ)
    out_row = iota((192, R), 0)
    back = iota((192, R), 1) == (out_row // 6) * 8 + out_row % 6
    states = mm(jnp.where(back, 1.0, 0.0).astype(BF), hid[...].reshape(R, 128))
    hid_out[...] = states[:, :DL].astype(BF)
    gathered(23, nrm, NZ)
    col = iota((128, 192), 1)
    norms = jnp.zeros((1, 192), F32)
    for i in range(NZ):
        at = (col // 6) * 8 + col % 6 - i * 32
        norms = norms + jnp.sum(
            jnp.where(iota((128, 192), 0) == at, to_col(nrm[i], 128), 0.0), axis=0, keepdims=True
        )
    norm_out[...] = norms

    @pl.when(p < TILES)
    def _():
        scattered(25, lp_r)
        logits = l_f[:, pl.ds(pl.multiple_of(p * 128, 128), 128)]
        for i in range(PLANE - 1):
            logits = logits + lp_r[i].astype(F32)
        top = jnp.max(logits, axis=1, keepdims=True)
        lane_h = iota((HC, 128), 1) - c * HC
        top = jnp.sum(jnp.where(lane_h == iota((HC, 128), 0), top, 0.0), axis=0, keepdims=True)
        lane_1 = iota((1, 128), 1) - c * HC
        mx_p[p, 0:1] = jnp.where((lane_1 >= 0) & (lane_1 < HC), top, LOW)

    @pl.when(p >= TILES)
    def _():
        mx_p[p, 0:1] = jnp.full((1, 128), LOW, F32)

    gather_p(30, mx_p)
    gathered(30, mx_p, PLANE)
    mx_z[pair, 0:1] = jnp.max(mx_p[:, 0:1], axis=0)
    mx_z[pair, 1:2] = jnp.sum(mx_p[:, 1:2], axis=0)
    gather(31, mx_z, pair, dev_pair, NP)
    gathered(31, mx_z, NP)
    best = jnp.max(mx_z[:, 0:1], axis=0)
    score_out[...] = (mx_z[0, 1:2] + mx_z[1, 1:2])[:, :CONT]
    top_out[...] = best[:, :CONT]

    @pl.when(p < TILES)
    def _():
        part = lp_s.at[pl.ds(0, TILES - 1)]
        pltpu.make_async_copy(part, part, ssem.at[25]).wait()

    @pl.when(p >= TILES)
    def _():
        pltpu.make_async_copy(lp_s, lp_s, ssem.at[25]).wait()

    for s, part in waits:
        pltpu.make_async_copy(part, part, ssem.at[s]).wait()


def per_device(
    token_ids,
    prompt_lengths,
    tail_lengths,
    prompt_of,
    page_table,
    prompt_keys,
    prompt_values,
    tail_keys,
    tail_values,
    norm_gain,
    norm_bias,
    qkv_weight,
    qkv_bias,
    out_weight,
    out_bias,
    embedding,
    score_weight,
):
    vm = pl.BlockSpec(memory_space=pltpu.VMEM)
    hbm = pl.BlockSpec(memory_space=pl.ANY)

    def b(*shape):
        return pltpu.VMEM(shape, BF)

    def f(*shape):
        return pltpu.VMEM(shape, F32)

    i32 = jnp.int32
    scratch = [
        pltpu.VMEM((1, 6), i32),
        pltpu.VMEM((2, CONT), i32),
        pltpu.VMEM((1, CONT), i32),
        pltpu.VMEM((1, CONT), i32),
        pltpu.VMEM((2, CONT), i32),
        b(2, DL),
        b(2, DL),
        b(3, 768),
        b(1, DL),
        b(1, DL),
        b(768, 768),
        b(768, 768),
        b(384, 768),
        b(384, 768),
        b(3, DL, 768),
        b(DL, 768),
        b(DL, VL),
        f(R, 1152),
        b(NC, R, 128),
        f(8, 128),
        b(8, 32, 128),
        b(7, 32, 128),
        b(NP, 32, 128),
        f(8, 128),
        b(3, DL, HALF),
        b(DL, VL),
        f(PLANE, 4, 128),
        f(NP, 4, 128),
        f(R, HALF),
        b(PLANE, 8, HALF),
        b(PLANE - 1, 8, HALF),
        b(PLANE, 8, HALF),
        b(NC, PLANE, 8, HALF),
        f(2, R, HALF),
        b(PLANE, 2, 8, HALF),
        b(PLANE - 1, 2, 8, HALF),
        f(2, R, HALF),
        f(2, R, 128),
        b(1, R, 512),
        b(1, R, 512),
        b(PLANE, 8, 512),
        b(PLANE - 1, 8, 512),
        b(PLANE, 8, HALF),
        b(NC, PLANE, 8, HALF),
        b(8, 32, 128),
        b(7, 32, 128),
        f(NC, 2, 128),
        f(PLANE, 2, 128),
        b(8, 32, 128),
        b(NP, 16, 128),
        f(NZ, 1, 128),
        f(HC, VL),
        b(TILES, HC, 128),
        b(PLANE - 1, HC, 128),
        f(PLANE, 2, 128),
        f(NP, 2, 128),
        pltpu.SemaphoreType.DMA((32,)),
        pltpu.SemaphoreType.DMA((32,)),
        pltpu.SemaphoreType.DMA((17,)),
    ]
    hidden, score, norms, top = pl.pallas_call(
        kernel,
        out_shape=(
            jax.ShapeDtypeStruct((192, DL), BF),
            jax.ShapeDtypeStruct((1, CONT), F32),
            jax.ShapeDtypeStruct((1, 192), F32),
            jax.ShapeDtypeStruct((1, CONT), F32),
        ),
        in_specs=[hbm] * 17,
        out_specs=(vm, vm, vm, vm),
        scratch_shapes=scratch,
        compiler_params=pltpu.CompilerParams(
            collective_id=0, has_side_effects=True, vmem_limit_bytes=60 * 2**20
        ),
    )(
        prompt_lengths.reshape(1, 6),
        token_ids.T,
        tail_lengths.reshape(1, CONT),
        prompt_of.reshape(1, CONT),
        page_table.T,
        norm_gain,
        norm_bias,
        qkv_bias,
        out_bias.reshape(1, DL),
        score_weight.reshape(1, DL),
        prompt_keys,
        prompt_values,
        tail_keys,
        tail_values,
        qkv_weight.transpose(1, 0, 2),
        out_weight.T,
        embedding.T,
    )
    return hidden, score.reshape(CONT), norms.reshape(192), top.reshape(CONT)


def solution(mesh):
    return jax.shard_map(
        per_device,
        mesh=mesh,
        in_specs=(
            P(),
            P(),
            P(),
            P(),
            P(),
            P("seq", "mp"),
            P("seq", "mp"),
            P("seq", "mp"),
            P("seq", "mp"),
            P(None, "seq"),
            P(None, "seq"),
            P("seq", None, "mp"),
            P(None, "mp"),
            P("mp", "seq"),
            P("seq"),
            P("mp", "seq"),
            P("seq"),
        ),
        out_specs=(P(None, "seq"), P(), P(), P()),
        check_vma=False,
    )
```
